32 devices in a mesh: wide: 8 (over y, x, core), narrow: 4 (over z).
Axes of the slice: x: 2, y: 2, z: 4, core: 2. Of those that a mesh axis runs over, the one named last changes fastest.
Arguments:
- target: bfloat16 [32768, 512], P(('wide', 'narrow')), may hold values from -6 to 6
- memory: bfloat16 [32768, 512], P(('wide', 'narrow')), may hold values from -6 to 6
- cotangent: bfloat16 [32768, 512], P(('wide', 'narrow')), may hold values from -6 to 6
- target_lengths: int32 [32, 27], P(('wide', 'narrow')), may hold values from 1 to 250, 1024 in all within a row
- source_lengths: int32 [32, 27], P(('wide', 'narrow')), may hold values from 1 to 250, 1024 in all within a row
- self_qkv: bfloat16 [512, 1536], P(('wide', 'narrow')), may hold values from -0.25 to 0.25
- self_out: bfloat16 [512, 512], P(('wide', 'narrow')), may hold values from -1 to 1
- self_bias: bfloat16 [3, 512], P(None, ('wide', 'narrow')), may hold values from -3 to 3
- cross_qkv: bfloat16 [512, 1536], P(('wide', 'narrow')), may hold values from -0.25 to 0.25
- cross_out: bfloat16 [512, 512], P(('wide', 'narrow')), may hold values from -1 to 1
- cross_bias: bfloat16 [3, 512], P(None, ('wide', 'narrow')), may hold values from -3 to 3
- ff_in: bfloat16 [512, 2048], P(('wide', 'narrow')), may hold values from -0.25 to 0.25
- ff_in_bias: bfloat16 [2048], P(('wide', 'narrow')), may hold values from -3 to 3
- ff_out: bfloat16 [2048, 512], P(('wide', 'narrow')), may hold values from -0.125 to 0.125
- ff_out_bias: bfloat16 [512], P(('wide', 'narrow')), may hold values from -3 to 3
- ln_gain: bfloat16 [3, 512], P(None, ('wide', 'narrow')), may hold values from 0.5 to 1.5
- ln_bias: bfloat16 [3, 512], P(None, ('wide', 'narrow')), may hold values from -3 to 3
Outputs:
- layer_output: bfloat16 [32768, 512], P(('wide', 'narrow'))
- target_grad: float32 [32768, 512], P(('wide', 'narrow'))
- memory_grad: float32 [32768, 512], P(('wide', 'narrow'))
- self_qkv_grad: float32 [512, 1536], P(('wide', 'narrow'))
- self_out_grad: float32 [512, 512], P(('wide', 'narrow'))
- self_bias_grad: float32 [3, 512], P(None, ('wide', 'narrow'))
- cross_qkv_grad: float32 [512, 1536], P(('wide', 'narrow'))
- cross_out_grad: float32 [512, 512], P(('wide', 'narrow'))
- cross_bias_grad: float32 [3, 512], P(None, ('wide', 'narrow'))
- ff_in_grad: float32 [512, 2048], P(('wide', 'narrow'))
- ff_in_bias_grad: float32 [2048], P(('wide', 'narrow'))
- ff_out_grad: float32 [2048, 512], P(('wide', 'narrow'))
- ff_out_bias_grad: float32 [512], P(('wide', 'narrow'))
- ln_gain_grad: float32 [3, 512], P(None, ('wide', 'narrow'))
- ln_bias_grad: float32 [3, 512], P(None, ('wide', 'narrow'))
The draws below stay inside these ranges and needn't reach their ends.
Inputs may be any that keep to these rules, and one draw needn't show every extreme that they name: `target_lengths`: each row sums to 1024, and its largest entry is 250. `source_lengths`: each row sums to 1024, and its largest entry is 250.
All inputs are finite; a program needn't handle non-finite values.
Results may differ from the reference program's by a relative error of at most 0.02.
Values may be sent and summed in bfloat16 or wider, within the bound.
A program may use at most 192 MiB of HBM per device.

```python
import math
import jax
import jax.numpy as jnp
import numpy as np
from jax import lax

D = 512
HEADS = 8
FF = 2048
HEAD = 64
TOK_DEV = 1024
MOST_LEN = 250
SEQ_DEV = 27
SRC_DEV = 1024
TOKENS = 32768
SOURCES = 32768
DEVICES = 32


def block_scale(rng, shape, pieces, smallest, top_value):
    level = 1.0
    for position, parts in pieces:
        steps = jax.random.uniform(jax.random.fold_in(jax.random.fold_in(rng, 6), position), (parts,), jnp.float32, smallest / len(pieces), top_value / len(pieces))
        level = level * jnp.repeat(jnp.exp(steps), shape[position] // parts).reshape((-1,) + (1,) * (len(shape) - 1 - position))
    return level


def split_up(number_of, total, most, skew):
    weights = [(1 << 20) // math.isqrt(standing ** skew) + 1 for standing in range(2, number_of + 1)]
    surplus, counts = total - most - (number_of - 1), [1] * (number_of - 1)
    while surplus > 0:
        movable = [i for i in range(number_of - 1) if counts[i] < most]
        whole, left = sum([weights[i] for i in movable]), surplus
        for i in movable:
            more = min(most - counts[i], max(1, left * weights[i] // whole), surplus)
            counts[i] = counts[i] + more
            surplus = surplus - more
    return np.array([most] + counts)


def uneven(own_key, number_of, total, bound, slope):
    if number_of == 2:
        one = jax.random.randint(own_key, (), max(1, total - bound), min(bound, total - 1) + 1)
        return jnp.stack([one, total - one])
    sizes = jnp.asarray(split_up(number_of, total, bound, slope), jnp.int32)
    couples = (number_of - 1) // 2
    giver, taker = sizes[1:1 + 2 * couples:2], sizes[2:2 + 2 * couples:2]
    room = jnp.minimum(giver - 1, bound - taker)
    shifted = jax.random.randint(jax.random.fold_in(own_key, 1), (couples,), 0, 1 << 20) % (room + 1)
    sizes = sizes.at[1:1 + 2 * couples:2].set(giver - shifted).at[2:2 + 2 * couples:2].set(taker + shifted)
    return sizes[jax.random.permutation(jax.random.fold_in(own_key, 2), number_of)]


def normal_values(stream_key, extent, scale, most, pieces=(), kind=jnp.bfloat16):
    values = jax.random.normal(stream_key, extent, jnp.float32) * scale
    if len(pieces) > 0:
        values = block_scale(stream_key, extent, pieces, -0.22, 0.18) * values
    return jnp.clip(values, min=-most, max=most).astype(kind)


def setup_inputs(seed: int = 0) -> dict:
    key_list = jax.random.split(jax.random.key(seed), 18)
    return {
        "target": normal_values(key_list[0], (TOKENS, D), 1.0, 6.0, ((0, 32),)),
        "memory": normal_values(key_list[1], (SOURCES, D), 1.0, 6.0, ((0, 32),)),
        "cotangent": normal_values(key_list[2], (TOKENS, D), 1.0, 6.0, ((0, 32),)),
        "target_lengths": jax.vmap(lambda own: uneven(own, SEQ_DEV, TOK_DEV, MOST_LEN, 2))(jax.random.split(key_list[3], DEVICES)).reshape((DEVICES, SEQ_DEV)).astype(jnp.int32),
        "source_lengths": jax.vmap(lambda own: uneven(own, SEQ_DEV, SRC_DEV, MOST_LEN, 2))(jax.random.split(key_list[4], DEVICES)).reshape((DEVICES, SEQ_DEV)).astype(jnp.int32),
        "self_qkv": normal_values(key_list[5], (D, 3 * D), D ** -0.5, 0.25, ((0, 32),)),
        "self_out": normal_values(key_list[6], (D, D), (D // 16) ** -0.5, 1.0, ((0, 32),)),
        "self_bias": normal_values(key_list[7], (3, D), 0.5, 3.0, ((1, 32),)),
        "cross_qkv": normal_values(key_list[8], (D, 3 * D), D ** -0.5, 0.25, ((0, 32),)),
        "cross_out": normal_values(key_list[9], (D, D), (D // 16) ** -0.5, 1.0, ((0, 32),)),
        "cross_bias": normal_values(key_list[10], (3, D), 0.5, 3.0, ((1, 32),)),
        "ff_in": normal_values(key_list[11], (D, FF), D ** -0.5, 0.25, ((0, 32),)),
        "ff_in_bias": normal_values(key_list[12], (FF,), 0.5, 3.0, ((0, 32),)),
        "ff_out": normal_values(key_list[13], (FF, D), FF ** -0.5, 0.125, ((0, 32),)),
        "ff_out_bias": normal_values(key_list[14], (D,), 0.5, 3.0, ((0, 32),)),
        "ln_gain": jnp.clip(1.0 + 0.1 * jax.random.normal(key_list[15], (3, D), jnp.float32), 0.5, 1.5).astype(jnp.bfloat16),
        "ln_bias": normal_values(key_list[16], (3, D), 0.5, 3.0, ((1, 32),)),
    }


EPSILON = 1e-05
MASKED = -1e+30
PRECISE = lax.Precision.HIGHEST

@jax.custom_vjp
def low(v):
    return lax.optimization_barrier(v.astype(jnp.bfloat16)).astype(jnp.float32)

@jax.custom_vjp
def low_back(v):
    return v

def low_keep(v):
    return (low(v), None)

def low_pass(kept, grad):
    return (grad,)

def back_keep(v):
    return (v, None)

def back_low(kept, grad):
    return (low(grad),)
low.defvjp(low_keep, low_pass)
low_back.defvjp(back_keep, back_low)

def project(left_side, right_side):
    return jnp.dot(left_side, right_side, precision=PRECISE)

def layer_norm(summed, gain, shift):
    centre = summed - lax.optimization_barrier(jnp.mean(summed, axis=-1, keepdims=True))
    spread = lax.optimization_barrier(jnp.mean(centre * centre, axis=-1, keepdims=True))
    return centre * lax.rsqrt(spread + EPSILON) * gain + shift

def segment_ids(lengths, row_count):
    ending = jnp.cumsum(lengths.astype(jnp.int32))
    places = jnp.arange(row_count, dtype=jnp.int32)
    return lax.optimization_barrier(jnp.sum((places[:, None] >= ending[None, :]).astype(jnp.int32), axis=1))

def attention(query, key_rows, value_rows, allowed):
    row_count = query.shape[0]
    query3 = query.reshape(row_count, HEADS, HEAD)
    key3 = key_rows.reshape(key_rows.shape[0], HEADS, HEAD)
    value3 = value_rows.reshape(value_rows.shape[0], HEADS, HEAD)
    scores = low_back(jnp.einsum('qhd,khd->hqk', query3, key3, precision=PRECISE) * HEAD ** (-0.5))
    scores = jnp.where(allowed[None], scores, MASKED)
    row_max = lax.optimization_barrier(jnp.max(scores, axis=2, keepdims=True))
    exponent = jnp.exp(scores - row_max)
    probability = low(exponent / lax.optimization_barrier(jnp.sum(exponent, axis=2, keepdims=True)))
    mixed_rows = jnp.einsum('hqk,khd->qhd', probability, value3, precision=PRECISE)
    return mixed_rows.reshape(row_count, HEADS * HEAD)

def block_forward(target, memory, target_lengths, source_lengths, weights):
    self_qkv, self_out, self_bias, cross_qkv, cross_out, cross_bias, ff_in, ff_in_bias, ff_out, ff_out_bias, ln_gain, ln_bias = weights
    row_count = target.shape[0]
    places = jnp.arange(row_count, dtype=jnp.int32)
    target_seg = segment_ids(target_lengths, row_count)
    source_seg = segment_ids(source_lengths, memory.shape[0])
    self_allowed = (target_seg[:, None] == target_seg[None, :]) & (places[None, :] <= places[:, None])
    cross_allowed = target_seg[:, None] == source_seg[None, :]
    packed = project(target, self_qkv)
    query = low(low_back(packed[:, :D]) + self_bias[0])
    key_rows = low(low_back(packed[:, D:2 * D]))
    value_rows = low(low_back(packed[:, 2 * D:]) + self_bias[1])
    attended = low(low_back(attention(query, key_rows, value_rows, self_allowed)))
    residual_one = target + (low_back(project(attended, self_out)) + self_bias[2])
    normed_one = layer_norm(residual_one, ln_gain[0], ln_bias[0])
    cross_query = low(low_back(project(low(normed_one), cross_qkv[:, :D])) + cross_bias[0])
    memory_pack = project(memory, cross_qkv[:, D:])
    cross_key = low(low_back(memory_pack[:, :D]))
    cross_value = low(low_back(memory_pack[:, D:]) + cross_bias[1])
    cross_att = low(low_back(attention(cross_query, cross_key, cross_value, cross_allowed)))
    residual_two = normed_one + (low_back(project(cross_att, cross_out)) + cross_bias[2])
    normed_two = layer_norm(residual_two, ln_gain[1], ln_bias[1])
    pre_act = low_back(project(low(normed_two), ff_in)) + ff_in_bias
    activated = low(jax.nn.gelu(pre_act))
    residual_three = normed_two + (low_back(project(activated, ff_out)) + ff_out_bias)
    return layer_norm(residual_three, ln_gain[2], ln_bias[2])

def reference(target, memory, cotangent, target_lengths, source_lengths, self_qkv, self_out, self_bias, cross_qkv, cross_out, cross_bias, ff_in, ff_in_bias, ff_out, ff_out_bias, ln_gain, ln_bias):
    floats = [operand.astype(jnp.float32) for operand in (target, memory, self_qkv, self_out, self_bias, cross_qkv, cross_out, cross_bias, ff_in, ff_in_bias, ff_out, ff_out_bias, ln_gain, ln_bias)]
    group_count = target.shape[0] // TOK_DEV

    def forward(target_full, memory_full, *weights):
        target_blocks = target_full.reshape(group_count, TOK_DEV, D)
        memory_blocks = memory_full.reshape(group_count, SRC_DEV, D)

        def one_group(carried, group_items):
            return (carried, block_forward(group_items[0], group_items[1], group_items[2], group_items[3], weights))
        _, outputs = lax.scan(jax.checkpoint(one_group), jnp.zeros((), jnp.float32), (target_blocks, memory_blocks, target_lengths, source_lengths))
        return outputs.reshape(target_full.shape)
    result, pullback = jax.vjp(forward, *floats)
    gradients = pullback(cotangent.astype(jnp.float32))
    return (result.astype(jnp.bfloat16), gradients[0], gradients[1], gradients[2], gradients[3], gradients[4], gradients[5], gradients[6], gradients[7], gradients[8], gradients[9], gradients[10], gradients[11], gradients[12], gradients[13])
```

```python
import functools
import math

import jax
import jax.numpy as jnp
from jax import lax
from jax.experimental import pallas as pl
from jax.experimental.pallas import tpu as pltpu
from jax.sharding import PartitionSpec as P

HEADS = 8
HEAD = 64
PAIRS = HEADS // 2
PAIR = 2 * HEAD
EPSILON = 1e-05
MASKED = -1e30
LINE = 128
TILE = 512
CHUNK = 512
VECTORS = 24
F32 = jnp.float32
BF16 = jnp.bfloat16
MESH = pl.DeviceIdType.MESH
VMEM_BYTES = 63 * 1024 * 1024

SELF_BIAS, CROSS_BIAS, GAIN, SHIFT, OUT_BIAS, IN_BIAS = 0, 3, 6, 9, 12, 13


def nn(left_side, right_side):
    return lax.dot_general(
        left_side, right_side, (((1,), (0,)), ((), ())), preferred_element_type=F32
    )


def nt(left_side, right_side):
    return lax.dot_general(
        left_side, right_side, (((1,), (1,)), ((), ())), preferred_element_type=F32
    )


def tn(left_side, right_side):
    return lax.dot_general(
        left_side, right_side, (((0,), (0,)), ((), ())), preferred_element_type=F32
    )


def part(step, size):
    if isinstance(step, int):
        return slice(step * size, (step + 1) * size)
    return pl.ds(pl.multiple_of(step * size, size), size)


def matrix(ref, first=0, columns=None):
    columns = ref.shape[-1] if columns is None else columns
    value = ref[:, :, :, :, first : first + columns]
    return value.reshape(-1, columns)


def loop(count, body, hooks=(), shift=0):
    def step(i, carry):
        body(i)
        for place, move in hooks:
            pl.when(i + shift == place)(move)
        return carry

    lax.fori_loop(0, count, step, 0)


def each(count, body):
    for i in range(count):
        body(i)


def hook(every, place, *moves):
    def move():
        for group, step in moves:
            every(group, step)

    return [(place, move)] if every is not None else []


def normalise(summed):
    centre = summed - jnp.mean(summed, axis=-1, keepdims=True)
    spread = jnp.mean(centre * centre, axis=-1, keepdims=True)
    scale = lax.rsqrt(spread + EPSILON)
    return centre * scale, scale


def normalise_back(grad, hat, scale, gain):
    inner = grad * gain
    first = jnp.mean(inner, axis=-1, keepdims=True)
    second = jnp.mean(inner * hat, axis=-1, keepdims=True)
    return (inner - first - hat * second) * scale


def column_sum(value):
    return jnp.sum(value, axis=0, keepdims=True)


def sentence_hits(lengths, rows):
    lane = lax.broadcasted_iota(jnp.int32, (1, LINE), 1)
    first = jnp.zeros((1, LINE), jnp.int32)
    last = jnp.zeros((1, LINE), jnp.int32)
    total = jnp.int32(0)
    for s in range(lengths.shape[1]):
        first = jnp.where(lane == s, total, first)
        total = total + lengths[0, s]
        last = jnp.where(lane == s, total, last)
    row = lax.broadcasted_iota(jnp.int32, (rows, LINE), 0)
    return (row >= first) & (row < last)


def twice(row):
    return jnp.concatenate([row, row], axis=1)


def beside(left_side, right_side):
    return jnp.concatenate([left_side, right_side], axis=1)


def stacked(value):
    lane = lax.broadcasted_iota(jnp.int32, (1, PAIR), 1)
    left = (lane < HEAD).astype(BF16)
    right = (lane >= HEAD).astype(BF16)
    return jnp.concatenate([value * left, value * right], axis=0)


def pair_row(ref, block, pair):
    return jnp.concatenate(
        [ref[block, pl.ds(2 * pair, 1), :], ref[block, pl.ds(2 * pair + 1, 1), :]], axis=1
    )


def diagonal(value):
    return jnp.concatenate([value[:HEAD, :LINE], value[HEAD:, LINE:]], axis=0)


def spread_rows(row):
    return jnp.concatenate(
        [
            jnp.broadcast_to(row[:, :LINE], (HEAD, LINE)),
            jnp.broadcast_to(row[:, LINE:], (HEAD, LINE)),
        ],
        axis=0,
    )


def keep_row(ref, block, pair, row):
    ref[block, pl.ds(2 * pair, 1), :] = row[:, :LINE]
    ref[block, pl.ds(2 * pair + 1, 1), :] = row[:, LINE:]


def score_back(probability, value_part, grad_block, delta):
    grad_prob = nt(value_part, grad_block) - delta
    return probability * grad_prob.astype(BF16)


def write_grad(grad_ref, delta_ref, portion, tile, grad_low, mixed_low):
    product = grad_low.astype(F32) * mixed_low.astype(F32)
    shape = (2 * HEADS, product.shape[1])
    head = lax.broadcasted_iota(jnp.int32, shape, 0) % HEADS
    owner = lax.broadcasted_iota(jnp.int32, shape, 1) // HEAD
    chosen = (head == owner).astype(BF16)
    high = product.astype(BF16)
    rest = (product - high.astype(F32)).astype(BF16)
    delta = (nt(chosen, high) + nt(chosen, rest))[:HEADS]
    for n in range(TILE // LINE):
        lines = slice(n * LINE, (n + 1) * LINE)
        block = tile * (TILE // LINE) + n
        by = portion[block]
        delta_ref[block] = delta[:, lines] * by
        high = by.astype(BF16)
        rest = (by - high.astype(F32)).astype(BF16)
        wide = tn(jnp.concatenate([high, rest], axis=0), chosen)
        grad_ref[part(block, LINE), :] = (grad_low[lines].astype(F32) * wide).astype(BF16)


def weight_grad(out_ref, left_ref, right_ref, first=0, start=0, count=None):
    rows = left_ref.shape[1]
    columns = right_ref.shape[1] if count is None else count
    wide = min(columns, CHUNK)
    piece = CHUNK
    blocks = out_ref.shape[3]

    def step(i):
        turned = left_ref[:, part(i, piece)].T

        def column(j):
            right = right_ref[:, pl.ds(pl.multiple_of(start + j * wide, LINE), wide)]
            value = nn(turned, right).astype(BF16)
            lanes = pl.ds(pl.multiple_of(first + j * wide, LINE), wide)
            if rows == piece:
                out_ref[:, :, :, :, lanes] = value.reshape(2, 2, 2, blocks, wide)
            else:
                out_ref[i // 2, i % 2, :, :, lanes] = value.reshape(2, blocks, wide)

        loop(columns // wide, column)

    loop(rows // piece, step)


class Copies:
    COUNT = 128

    def __init__(self, sems):
        self.sems, self.used, self.open = sems, 0, {}

    def start(self, source, target):
        number = self.used
        self.used += 1
        self.open[number] = pltpu.make_async_copy(source, target, self.sems.at[number])
        self.open[number].start()
        return number

    def tiles(self, source, target, count, size):
        return Tiles(self, source, target, count, size)

    def wait(self, *numbers):
        for number in numbers:
            if number in self.open:
                self.open.pop(number).wait()

    def close(self):
        self.wait(*list(self.open))


class Tiles:
    def __init__(self, owner, source, target, count, size):
        self.source, self.target, self.size, self.count = source, target, size, count
        self.sems, self.first = owner.sems, owner.used
        owner.used += count

    def copy(self, i):
        lines = part(i, self.size)
        return pltpu.make_async_copy(
            self.source.at[lines], self.target.at[lines], self.sems.at[self.first + i]
        )

    def start(self, i):
        self.copy(i).start()

    def start_all(self):
        for i in range(self.count):
            self.start(i)

    def wait(self, i):
        self.copy(i).wait()

    def wait_all(self):
        for i in range(self.count):
            self.wait(i)


class Kept:
    SLOTS = 2

    def __init__(self, owner, far_ref, made, back):
        self.far, self.made, self.back = far_ref, made, back
        self.count, self.rows, self.lanes = far_ref.shape
        self.sems, self.out, self.into = owner.sems, owner.used, owner.used + self.count
        owner.used += 2 * self.count

    def place(self, t, p=0, lanes=2 * LINE):
        start = t % self.SLOTS * (self.made.shape[1] // self.SLOTS) + p * 2 * LINE
        return pl.ds(pl.multiple_of(start, 2 * LINE), lanes)

    def slot(self, buffer, t):
        return buffer.at[pl.ds(0, self.rows), self.place(t, 0, self.lanes)]

    def leaving(self, t):
        return pltpu.make_async_copy(
            self.slot(self.made, t), self.far.at[t], self.sems.at[self.out + t]
        )

    def coming(self, t):
        return pltpu.make_async_copy(
            self.far.at[t], self.slot(self.back, t), self.sems.at[self.into + t]
        )

    def make_room(self, t):
        @pl.when(t >= self.SLOTS)
        def _():
            self.leaving(t - self.SLOTS).wait()

    def all_left(self):
        for t in range(self.count - self.SLOTS, self.count):
            self.leaving(t).wait()

    def open(self):
        for t in range(self.SLOTS):
            self.coming(t).start()

    def next(self, t):
        @pl.when(t + self.SLOTS < self.count)
        def _():
            self.coming(t + self.SLOTS).start()


class Place:
    def __init__(self, narrow):
        self.narrow = narrow
        wide = lax.axis_index("wide")
        self.z = lax.axis_index("narrow")
        self.y = wide // 4
        self.x = (wide // 2) % 2
        self.c = wide % 2
        self.other_y = 1 - self.y
        self.other_x = 1 - self.x
        self.other_c = 1 - self.c
        self.index = wide * narrow + self.z
        self.core_peer = (self.y * 4 + self.x * 2 + self.other_c, self.z)
        self.x_peer = (self.y * 4 + self.other_x * 2 + self.c, self.z)
        self.y_peer = (self.other_y * 4 + self.x * 2 + self.c, self.z)
        self.z_places = [lax.rem(self.z + k, narrow) for k in range(1, narrow)]
        self.z_from = [lax.rem(self.z + narrow - k, narrow) for k in range(1, narrow)]
        self.z_peers = [(wide, there) for there in self.z_places]

    def greet(self):
        barrier = pltpu.get_barrier_semaphore()
        peers = [self.core_peer, self.x_peer, self.y_peer] + self.z_peers
        for peer in peers:
            pl.semaphore_signal(barrier, inc=1, device_id=peer, device_id_type=MESH)
        return lambda: pl.semaphore_wait(barrier, len(peers))


class Gather:
    def __init__(self, at, shard, full, send, recv, number, copies):
        self.at, self.shard, self.full, self.copies = at, shard, full, copies
        self.send, self.recv, self.number = send, recv, number
        self.rows = shard.shape[0]
        self.half = shard.shape[0] * at.narrow // 2

    def copy(self, slot, source, target, peer):
        return pltpu.make_async_remote_copy(
            src_ref=source,
            dst_ref=target,
            send_sem=self.send.at[self.number, slot],
            recv_sem=self.recv.at[self.number, slot],
            device_id=peer,
            device_id_type=MESH,
        )

    def go(self, slot, region, peer, source=None):
        self.copy(slot, region if source is None else source, region, peer).start()

    def arrive(self, slot, region, peer):
        self.copy(slot, region, region, peer).wait_recv()

    def line(self, z):
        at = self.at
        rows = pl.ds(pl.multiple_of(z * self.rows, self.rows), self.rows)
        return self.full.at[at.y, at.x, at.c, rows]

    def begin(self):
        at = self.at
        for k in range(at.narrow - 1):
            self.go(k, self.line(at.z), at.z_peers[k], self.shard)
        self.own = self.copies.start(self.shard, self.line(at.z))

    def second(self):
        at, full, h = self.at, self.full, self.half
        self.copies.wait(self.own)
        for k in range(at.narrow - 1):
            self.arrive(k, self.line(at.z_from[k]), at.z_peers[k])
        n = at.narrow - 1
        self.go(n, full.at[at.y, at.x, at.c, pl.ds(0, h)], at.x_peer)
        self.go(n + 1, full.at[at.y, at.x, at.c, pl.ds(h, h)], at.y_peer)

    def third(self):
        at, full, h = self.at, self.full, self.half
        n = at.narrow - 1
        self.arrive(n, full.at[at.y, at.other_x, at.c, pl.ds(0, h)], at.x_peer)
        self.go(n + 2, full.at[at.y, :, at.c, pl.ds(0, h)], at.y_peer)
        self.arrive(n + 1, full.at[at.other_y, at.x, at.c, pl.ds(h, h)], at.y_peer)
        self.go(n + 3, full.at[:, at.x, at.c, pl.ds(h, h)], at.x_peer)

    def fourth(self):
        at, full, h = self.at, self.full, self.half
        n = at.narrow - 1
        self.arrive(n + 2, full.at[at.other_y, :, at.c, pl.ds(0, h)], at.y_peer)
        self.arrive(n + 3, full.at[:, at.other_x, at.c, pl.ds(h, h)], at.x_peer)
        self.go(n + 4, full.at[:, :, at.c], at.core_peer)

    def last(self):
        at, full = self.at, self.full
        self.arrive(at.narrow + 3, full.at[:, :, at.other_c], at.core_peer)

    def close(self):
        at, full, h, n = self.at, self.full, self.half, self.at.narrow - 1
        sent = [self.line(at.z)] * n
        sent += [full.at[at.y, at.x, at.c, pl.ds(0, h)], full.at[at.y, at.x, at.c, pl.ds(h, h)]]
        sent += [full.at[at.y, :, at.c, pl.ds(0, h)], full.at[:, at.x, at.c, pl.ds(h, h)]]
        sent += [full.at[:, :, at.c]]
        for slot, region in enumerate(sent):
            self.copy(slot, region, region, at.core_peer).wait_send()


class Scatter:
    SCRATCH = 6

    def __init__(self, at, grad, out, buffers, send, recv, number):
        self.at, self.grad, self.out = at, grad, out
        self.total, self.in_a, self.in_b, self.in_a2, self.in_b2, self.in_z = buffers
        self.send, self.recv, self.number = send, recv, number
        self.rows = out.shape[0]
        self.half = out.shape[0] * at.narrow // 2
    @staticmethod
    def scratch(rows, columns, narrow):
        block = rows * narrow
        h = block // 2
        return [
            pltpu.VMEM((2, 2, block, columns), BF16),
            pltpu.VMEM((2, h, columns), BF16),
            pltpu.VMEM((2, h, columns), BF16),
            pltpu.VMEM((h, columns), BF16),
            pltpu.VMEM((h, columns), BF16),
            pltpu.VMEM((narrow - 1, rows, columns), BF16),
        ]

    def copy(self, slot, source, target, peer):
        return pltpu.make_async_remote_copy(
            src_ref=source,
            dst_ref=target,
            send_sem=self.send.at[self.number, slot],
            recv_sem=self.recv.at[self.number, slot],
            device_id=peer,
            device_id_type=MESH,
        )

    def go(self, slot, source, target, peer):
        self.copy(slot, source, target, peer).start()

    def arrive(self, slot, target, peer):
        self.copy(slot, target, target, peer).wait_recv()

    def add(self, y, x, first, extra, index):
        size = 32

        def step(i):
            rows = pl.ds(pl.multiple_of(first + i * size, size), size)
            more = extra[(*index, pl.ds(pl.multiple_of(i * size, size), size))]
            made = self.total[y, x, rows, :].astype(F32) + more.astype(F32)
            self.total[y, x, rows, :] = made.astype(BF16)

        loop(extra.shape[-2] // size, step)

    def begin(self):
        at = self.at
        self.go(0, self.grad.at[:, :, at.other_c], self.total, at.core_peer)

    def second(self):
        at, h = self.at, self.half
        self.arrive(0, self.total, at.core_peer)
        loop(4, lambda t: self.add(t // 2, t % 2, 0, self.grad, (t // 2, t % 2, at.c)))
        self.go(1, self.total.at[at.other_y, :, pl.ds(0, h)], self.in_a, at.y_peer)
        self.go(2, self.total.at[:, at.other_x, pl.ds(h, h)], self.in_b, at.x_peer)

    def third(self):
        at, h = self.at, self.half
        self.arrive(1, self.in_a, at.y_peer)
        self.add(at.y, at.other_x, 0, self.in_a, (at.other_x,))
        self.go(3, self.total.at[at.y, at.other_x, pl.ds(0, h)], self.in_a2, at.x_peer)
        self.arrive(2, self.in_b, at.x_peer)
        self.add(at.other_y, at.x, h, self.in_b, (at.other_y,))
        self.go(4, self.total.at[at.other_y, at.x, pl.ds(h, h)], self.in_b2, at.y_peer)
        self.add(at.y, at.x, 0, self.in_a, (at.x,))
        self.add(at.y, at.x, h, self.in_b, (at.y,))

    def line(self, z):
        rows = pl.ds(pl.multiple_of(z * self.rows, self.rows), self.rows)
        return self.total.at[self.at.y, self.at.x, rows]

    def fourth(self):
        at, h = self.at, self.half
        self.arrive(3, self.in_a2, at.x_peer)
        self.add(at.y, at.x, 0, self.in_a2, ())
        self.arrive(4, self.in_b2, at.y_peer)
        self.add(at.y, at.x, h, self.in_b2, ())
        for k in range(at.narrow - 1):
            self.go(5 + k, self.line(at.z_places[k]), self.in_z.at[k], at.z_peers[k])

    def last(self):
        at = self.at
        rows = pl.ds(pl.multiple_of(at.z * self.rows, self.rows), self.rows)
        summed = self.total[at.y, at.x, rows, :].astype(F32)
        for k in range(at.narrow - 1):
            self.arrive(5 + k, self.in_z.at[k], at.z_peers[k])
            summed = summed + self.in_z[k].astype(F32)
        self.out[...] = summed

    def close(self):
        at, total, h = self.at, self.total, self.half
        sent = [self.grad.at[:, :, at.other_c]]
        sent += [total.at[at.other_y, :, pl.ds(0, h)], total.at[:, at.other_x, pl.ds(h, h)]]
        sent += [
            total.at[at.y, at.other_x, pl.ds(0, h)],
            total.at[at.other_y, at.x, pl.ds(h, h)],
        ]
        sent += [self.line(z) for z in at.z_places]
        for slot, region in enumerate(sent):
            self.copy(slot, region, region, at.core_peer).wait_send()


def unpack_vectors(vec_ref, full_ref, narrow):
    packed = matrix(full_ref)
    rows, lanes = packed.shape
    devices = rows // 16
    width = 512
    shape = (lanes, width)
    source = lax.broadcasted_iota(jnp.int32, shape, 0)
    place = lax.broadcasted_iota(jnp.int32, shape, 1)
    each = width // devices
    wide = (4 * width) // devices
    short = nn(packed, (source == place % each).astype(BF16))
    long = nn(packed, (source == place % wide).astype(BF16))
    shape = (rows, width)
    row = lax.broadcasted_iota(jnp.int32, shape, 0)
    lane = lax.broadcasted_iota(jnp.int32, shape, 1)
    short = jnp.where(row // 16 == lane // each, short, 0.0)
    kept = (row % 16 == IN_BIAS) & ((row // 16) % (devices // 4) == lane // wide)
    long = jnp.where(kept, long, 0.0)
    vec_ref[0:16, :] = jnp.sum(short.reshape(devices, 16, width), axis=0)
    for a in range(4):
        vec_ref[IN_BIAS + a : IN_BIAS + a + 1, :] = column_sum(
            long[a * rows // 4 : (a + 1) * rows // 4, :]
        )


WEIGHTS = 6
GATHERED = 9
SCATTERED = 5 + PAIRS
KEYS = 512
GROUP = 4
REACH = 3


def layer_kernel(exchange, narrow, *refs):
    refs = list(refs)
    take = lambda n: [refs.pop(0) for _ in range(n)]
    lengths, source_lengths, target_far, memory_far, cotangent_far = take(5)
    weights_far = take(WEIGHTS)
    if exchange:
        short_parts = take(6)
    else:
        (vec,) = take(1)
    output_far, memory_grad_far, target_grad_far = take(3)
    if exchange:
        outs = take(SCATTERED)
        (row_total,) = take(1)
    if exchange:
        self_far, cross_far = take(2)
        grads = take(4)
        (sums,) = take(1)
    else:
        grads = take(6)
        (sums,) = take(1)
        self_far, cross_far = take(2)
    weights = take(WEIGHTS)
    s_qkv, s_out, c_qkv, c_out, ff_in, ff_out = weights
    target, memory, cotangent, query, keys, values, mixed = take(7)
    cross_query, cross_key, cross_value, cross_mixed, hat, scale = take(6)
    turned, target_hit, source_hit, target_miss = take(4)
    activated, grad_pre_low, normed_low, low_three, low_two, grad_mixed, delta = take(7)
    portion, cross_portion, blocks, grad_blocks = take(4)
    grad, dk, dv, scale_two, local_sems = take(5)
    rows, width = target.shape
    if exchange:
        c_qkv_grad, c_out_grad, s_out_grad, s_parts = grads
        ff_out_grad, ff_in_grad = ff_out, ff_in
        grads = [ff_out_grad, ff_in_grad, c_qkv_grad, c_out_grad, s_out_grad]
        grads += [s_parts.at[n] for n in range(PAIRS)]
    else:
        ff_out_grad, ff_in_grad, c_qkv_grad, c_out_grad, s_out_grad, s_parts = grads
    sources = memory.shape[0]
    hidden = ff_in.shape[-1]
    steps = rows // TILE
    lines_count = rows // LINE
    copies = Copies(local_sems)
    self_kept = Kept(copies, self_far, activated, grad_pre_low)
    cross_kept = Kept(copies, cross_far, activated, grad_pre_low)

    if exchange:
        vec, short_full, short_wide, short, send, recv = take(6)
        buffers = [take(Scatter.SCRATCH) for _ in range(SCATTERED)]
        row_send, row_recv, s_send, s_recv, v_send, v_recv = take(6)
        at = Place(narrow)
        pairs = [(short, short_full)]
        for n in range(3):
            lanes = pl.ds(n * width, width)
            pairs.append((weights_far[0].at[:, lanes], s_qkv.at[:, :, :, :, lanes]))
        pairs += list(zip(weights_far[1:], weights[1:]))
        moves = [
            Gather(at, shard, full, send, recv, n, copies) for n, (shard, full) in enumerate(pairs)
        ]
        first, second, third = moves[0:4], moves[4:6], moves[6:9]
        sums_out = [
            Scatter(at, grads[n], outs[n], buffers[n], s_send, s_recv, n) for n in range(SCATTERED)
        ]
        ff_sum, cross_sum, out_sum = sums_out[0:2], sums_out[2:4], sums_out[4:5]
        part_sums = [sums_out[5 + n : 6 + n] for n in range(PAIRS)]

        def every(group, step):
            for move in group:
                getattr(move, step)()

        at_step = functools.partial(hook, every)
        all_here = at.greet()
        short_wide[...] = jnp.zeros_like(short_wide)
        row = 0
        for piece in short_parts:
            count, lanes = piece.shape
            short_wide[row : row + count, 0:lanes] = piece[...].astype(F32)
            row += count
        short[...] = short_wide[...].astype(BF16)
        all_here()
    else:
        first = second = third = ff_sum = cross_sum = out_sum = []
        part_sums = [[]] * PAIRS
        every = lambda group, step: None
        at_step = functools.partial(hook, None)

    every(first, "begin")
    loads = [copies.start(target_far, target)]
    later = [copies.start(memory_far, memory), copies.start(cotangent_far, cotangent)]
    if not exchange:
        for far_ref, near in zip(weights_far, weights):
            loads.append(copies.start(far_ref, near))
    hit = sentence_hits(lengths, rows)
    lane = lax.broadcasted_iota(jnp.int32, (rows, LINE), 1)
    target_hit[...] = jnp.where(hit, 1.0, 0.0).astype(BF16)
    target_miss[...] = jnp.where(hit | (lane >= lengths.shape[1]), 0.0, MASKED).astype(BF16)
    source_hit[...] = jnp.where(sentence_hits(source_lengths, sources), 1.0, 0.0).astype(BF16)
    sums[...] = jnp.zeros_like(sums)
    every(first, "second")
    every(second, "begin")
    every(first, "third")
    every(third, "begin")
    every(first, "fourth")
    every(second, "second")
    every(first, "last")
    if exchange:
        unpack_vectors(vec, short_full, narrow)
    copies.wait(*loads)

    def vector(row):
        return vec[row : row + 1, :]

    def add_sum(row, value):
        sums[row : row + 1, :] += column_sum(value)

    def project(i):
        lines = part(i, TILE)
        given = target[lines, :]
        made = nn(given, matrix(s_qkv, 0, width)) + vector(SELF_BIAS)
        query[lines, :] = (made * HEAD**-0.5).astype(BF16)
        keys[lines, :] = nn(given, matrix(s_qkv, width, width)).astype(BF16)
        made = nn(given, matrix(s_qkv, 2 * width, width)) + vector(SELF_BIAS + 1)
        low = made.astype(BF16)
        values[lines, :] = low
        turned[:, lines] = low.T

    each(steps, project)
    every(second, "third")
    every(third, "second")

    def query_block(ref, lines, lanes):
        missing = target_miss[lines, :]
        return beside(stacked(ref[lines, lanes]), jnp.concatenate([missing, missing], axis=0))

    def reach(i):
        return range(max(i - REACH + 1, 0), i + 1)

    def pair_lanes(pair):
        return pl.ds(pl.multiple_of(pair * PAIR, PAIR), PAIR)

    def rows_of(blocks_met):
        return slice(blocks_met[0] * LINE, (blocks_met[-1] + 1) * LINE)

    key_place = lax.broadcasted_iota(jnp.int32, (LINE, 2 * LINE), 0)
    query_place = lax.broadcasted_iota(jnp.int32, (LINE, 2 * LINE), 1) % LINE

    def attend(pair):
        lanes = pair_lanes(pair)
        self_kept.make_room(pair)
        for i in range(lines_count):
            lines, met = slice(i * LINE, (i + 1) * LINE), reach(i)
            span = rows_of(met)
            given = beside(keys[span, lanes], target_hit[span, :])
            scores = nt(given, query_block(query, lines, lanes))
            last = (len(met) - 1) * LINE
            pieces = [jnp.where(key_place <= query_place, scores[last:], MASKED)]
            if last:
                pieces.insert(0, scores[:last])
            tops = [jnp.max(value, axis=0, keepdims=True) for value in pieces]
            top = functools.reduce(jnp.maximum, tops)
            pieces = [jnp.exp(value - top) for value in pieces]
            by = 1.0 / sum(column_sum(value) for value in pieces)
            exponent = jnp.concatenate([value.astype(BF16) for value in pieces], axis=0)
            for n, k in enumerate(met):
                place = self_kept.place(pair, i - k)
                activated[k * LINE : (k + 1) * LINE, place] = exponent[n * LINE : (n + 1) * LINE]
            made = diagonal(nn(turned[lanes, span], exponent)) * spread_rows(by)
            mixed[lines, lanes] = made.T.astype(BF16)
            keep_row(portion, i, pair, by)
        self_kept.leaving(pair).start()

    loop(PAIRS, attend, at_step(0, (second, "fourth")) + at_step(1, (third, "third")))
    self_kept.all_left()
    every(second, "last")
    copies.wait(*later)

    def close_self(i):
        lines = part(i, TILE)
        summed = target[lines, :].astype(F32) + nn(mixed[lines, :], matrix(s_out))
        made, by = normalise(summed + vector(SELF_BIAS + 2))
        hat[lines, :] = made
        scale[lines, :] = jnp.broadcast_to(by, (TILE, LINE))
        normed = (made * vector(GAIN) + vector(SHIFT)).astype(BF16)
        made = nn(normed, matrix(c_qkv, 0, width)) + vector(CROSS_BIAS)
        cross_query[lines, :] = (made * HEAD**-0.5).astype(BF16)
        given = memory[lines, :]
        cross_key[lines, :] = nn(given, matrix(c_qkv, width, width)).astype(BF16)
        made = nn(given, matrix(c_qkv, 2 * width, width)) + vector(CROSS_BIAS + 1)
        low = made.astype(BF16)
        cross_value[lines, :] = low
        turned[:, lines] = low.T

    each(steps, close_self)

    groups = lines_count // GROUP
    cross_steps = PAIRS * groups

    def attend_cross(t):
        pair, group = t // groups, t % groups
        lanes = pair_lanes(pair)
        cross_kept.make_room(t)
        for n in range(GROUP):
            i = group * GROUP + n
            lines = part(i, LINE)
            block = query_block(cross_query, lines, lanes)
            scores = []
            for c in range(sources // KEYS):
                span = slice(c * KEYS, (c + 1) * KEYS)
                scores.append(nt(beside(cross_key[span, lanes], source_hit[span, :]), block))
            tops = [jnp.max(value, axis=0, keepdims=True) for value in scores]
            top = functools.reduce(jnp.maximum, tops)
            exponents = [jnp.exp(value - top) for value in scores]
            by = 1.0 / sum(column_sum(value) for value in exponents)
            exponent = jnp.concatenate([value.astype(BF16) for value in exponents], axis=0)
            activated[:, cross_kept.place(t, n)] = exponent
            made = diagonal(nn(turned[lanes, :], exponent)) * spread_rows(by)
            cross_mixed[lines, lanes] = made.T.astype(BF16)
            keep_row(cross_portion, i, pair, by)
        cross_kept.leaving(t).start()

    loop(cross_steps, attend_cross, at_step(cross_steps // 2 - 1, (third, "fourth")))
    cross_kept.all_left()
    every(third, "last")

    hat_two, slope = dk, grad_pre_low
    parts = hidden // CHUNK

    def open_feed(i):
        lines = part(i, TILE)
        normed_one = hat[lines, :] * vector(GAIN) + vector(SHIFT)
        summed = normed_one + nn(cross_mixed[lines, :], matrix(c_out)) + vector(CROSS_BIAS + 2)
        made, by = normalise(summed)
        hat_two[lines, :] = made
        scale_two[lines, :] = jnp.broadcast_to(by, (TILE, LINE))
        normed_low[lines, :] = (made * vector(GAIN + 1) + vector(SHIFT + 1)).astype(BF16)

    def feed_in(j, i):
        lines, lanes = part(i, TILE), part(j, CHUNK)
        weight = ff_in[:, :, :, :, lanes].reshape(width, CHUNK)
        u = nn(normed_low[lines, :], weight) + vec[pl.ds(IN_BIAS + j, 1), :]
        c0 = math.sqrt(2.0 / math.pi)
        square = u * u
        rise = 0.5 + 0.5 * jnp.tanh(u * (c0 + (c0 * 0.044715) * square))
        made = u * rise
        activated[lines, lanes] = made.astype(BF16)
        rate = rise + made * (1.0 - rise) * (2.0 * c0 + (6.0 * c0 * 0.044715) * square)
        slope[lines, lanes] = rate.astype(BF16)

    def feed_out(i):
        lines = part(i, TILE)
        normed_two = hat_two[lines, :] * vector(GAIN + 1) + vector(SHIFT + 1)
        summed = normed_two + nn(activated[lines, :], matrix(ff_out)) + vector(OUT_BIAS)
        hat_three, scale_three = normalise(summed)
        given = cotangent[lines, :].astype(F32)
        cotangent[lines, :] = (hat_three * vector(GAIN + 2) + vector(SHIFT + 2)).astype(BF16)
        add_sum(GAIN + 2, given * hat_three)
        add_sum(SHIFT + 2, given)
        grad_three = normalise_back(given, hat_three, scale_three, vector(GAIN + 2))
        add_sum(OUT_BIAS, grad_three)
        low_three[lines, :] = grad_three.astype(BF16)
        grad[lines, :] = grad_three

    def back_out(j, i):
        lines, lanes = part(i, TILE), part(j, CHUNK)
        weight = ff_out[j // 2, j % 2].reshape(CHUNK, width)
        grad_pre = nt(low_three[lines, :], weight) * slope[lines, lanes].astype(F32)
        sums[pl.ds(IN_BIAS + j, 1), :] += column_sum(grad_pre)
        grad_pre_low[lines, lanes] = grad_pre.astype(BF16)

    def back_in(i):
        lines = part(i, TILE)
        given = grad[lines, :] + nt(grad_pre_low[lines, :], matrix(ff_in))
        made = hat_two[lines, :]
        add_sum(GAIN + 1, given * made)
        add_sum(SHIFT + 1, given)
        grad_two = normalise_back(given, made, scale_two[lines, 0:1], vector(GAIN + 1))
        add_sum(CROSS_BIAS + 2, grad_two)
        grad[lines, :] = grad_two
        low = grad_two.astype(BF16)
        low_two[lines, :] = low
        mixed_grad = nt(low, matrix(c_out)).astype(BF16)
        write_grad(grad_mixed, delta, cross_portion, i, mixed_grad, cross_mixed[lines, :])

    if exchange:
        for move in moves:
            move.close()
    each(steps, open_feed)
    loop(parts, lambda j: each(steps, functools.partial(feed_in, j)))
    loop(steps, feed_out)
    copies.start(cotangent, output_far)
    loop(parts, lambda j: each(steps, functools.partial(back_out, j)))
    weight_grad(ff_out_grad, activated, low_three)
    every(ff_sum[:1], "begin")
    loop(steps, back_in)
    weight_grad(ff_in_grad, normed_low, grad_pre_low)
    every(ff_sum[1:], "begin")
    weight_grad(c_out_grad, cross_mixed, low_two)
    every(cross_sum[1:], "begin")

    dq = activated.at[:, 0:width]
    cross_dk_low, cross_dv_low = normed_low, cross_mixed
    cross_kept.open()

    def clear(i):
        lines = part(i, TILE)
        dk[lines, :] = jnp.zeros((TILE, width), F32)
        dv[lines, :] = jnp.zeros((TILE, width), F32)

    def turn(ref):
        def step(i):
            lines = part(i, TILE)
            turned[:, lines] = ref[lines, :].T

        return step

    loop(steps, clear)
    loop(steps, turn(cross_key))
    every(ff_sum, "second")

    grad_scores = activated.at[:, 2 * width : 4 * width]

    def attend_cross_back(t):
        pair, group = t // groups, t % groups
        lanes = pair_lanes(pair)
        places = [slice(n * 2 * LINE, (n + 1) * 2 * LINE) for n in range(GROUP)]
        for n, place in enumerate(places):
            lines = part(group * GROUP + n, LINE)
            blocks[place, :] = stacked(cross_query[lines, lanes])
            grad_blocks[place, :] = stacked(grad_mixed[lines, lanes])
        cross_kept.coming(t).wait()

        def some_keys(c):
            span = slice(c * KEYS, (c + 1) * KEYS)
            for n, place in enumerate(places):
                grad_scores[span, place] = score_back(
                    grad_pre_low[span, cross_kept.place(t, n)],
                    cross_value[span, lanes],
                    grad_blocks[place, :],
                    pair_row(delta, group * GROUP + n, pair),
                )
            kept = grad_pre_low[span, cross_kept.place(t, 0, cross_kept.lanes)]
            dv[span, lanes] += nn(kept, grad_blocks[0 : cross_kept.lanes, :])
            dk[span, lanes] += nn(grad_scores[span, :], blocks[0 : cross_kept.lanes, :])

        for c in range(sources // KEYS):
            some_keys(c)
        for n, place in enumerate(places):
            made = diagonal(nn(turned[lanes, :], grad_scores[:, place])).T * HEAD**-0.5
            sums[CROSS_BIAS : CROSS_BIAS + 1, lanes] += column_sum(made)
            dq[part(group * GROUP + n, LINE), lanes] = made.astype(BF16)
        cross_kept.next(t)

    loop(
        cross_steps,
        attend_cross_back,
        at_step(cross_steps // 4, (ff_sum, "third"))
        + at_step(cross_steps * 5 // 8, (cross_sum[1:], "second"), (ff_sum, "fourth")),
    )
    every(cross_sum[1:], "third")

    def close_cross(i):
        lines = part(i, TILE)
        made = dv[lines, :]
        add_sum(CROSS_BIAS + 1, made)
        cross_dv_low[lines, :] = made.astype(BF16)
        cross_dk_low[lines, :] = dk[lines, :].astype(BF16)
        low_three[lines, :] = (hat[lines, :] * vector(GAIN) + vector(SHIFT)).astype(BF16)

    self_kept.open()
    each(steps, close_cross)
    weight_grad(c_qkv_grad, low_three, dq, 0)
    weight_grad(c_qkv_grad, memory, cross_dk_low, width)
    weight_grad(c_qkv_grad, memory, cross_dv_low, 2 * width)
    every(cross_sum[:1], "begin")
    every(cross_sum[1:], "fourth")

    def open_self(i):
        lines = part(i, TILE)
        given = grad[lines, :] + nt(dq[lines, :], matrix(c_qkv, 0, width))
        made = hat[lines, :]
        add_sum(GAIN, given * made)
        add_sum(SHIFT, given)
        grad_one = normalise_back(given, made, scale[lines, 0:1], vector(GAIN))
        add_sum(SELF_BIAS + 2, grad_one)
        grad[lines, :] = grad_one
        low = grad_one.astype(BF16)
        low_two[lines, :] = low
        mixed_grad = nt(low, matrix(s_out)).astype(BF16)
        write_grad(grad_mixed, delta, portion, i, mixed_grad, mixed[lines, :])
        turned[:, lines] = keys[lines, :].T

    each(steps, open_self)
    every(cross_sum[:1], "second")
    weight_grad(s_out_grad, mixed, low_two)
    every(out_sum, "begin")
    all_grads = activated.at[:, 0 : 3 * width]

    def score_place(k, n):
        rows_here = slice(k * LINE, (k + 1) * LINE)
        if n < 2:
            return low_three.at[rows_here, n * 2 * LINE : (n + 1) * 2 * LINE]
        return low_two.at[rows_here, 0 : 2 * LINE]

    def attend_back(pair):
        lanes = pair_lanes(pair)

        def own(n):
            return pl.ds(pl.multiple_of(pair * 3 * PAIR + n * PAIR, PAIR), PAIR)

        for i in range(lines_count):
            lines = slice(i * LINE, (i + 1) * LINE)
            place = slice(i * 2 * LINE, (i + 1) * 2 * LINE)
            blocks[place, :] = stacked(query[lines, lanes])
            grad_blocks[place, :] = stacked(grad_mixed[lines, lanes])
        less = [pair_row(delta, i, pair) for i in range(lines_count)]
        self_kept.coming(pair).wait()
        value_sum = jnp.zeros((1, PAIR), F32)
        for k in range(lines_count):
            lines = slice(k * LINE, (k + 1) * LINE)
            count = min(REACH, lines_count - k)
            place = slice(k * 2 * LINE, (k + count) * 2 * LINE)
            exponent = grad_pre_low[lines, self_kept.place(pair, 0, count * 2 * LINE)]
            block, grad_block = blocks[place, :], grad_blocks[place, :]
            grad_score = score_back(
                exponent,
                values[lines, lanes],
                grad_block,
                jnp.concatenate(less[k : k + count], axis=1),
            )
            for n in range(count):
                score_place(k, n)[...] = grad_score[:, n * 2 * LINE : (n + 1) * 2 * LINE]
            made = nn(exponent, grad_block)
            value_sum = value_sum + column_sum(made)
            all_grads[lines, own(2)] = made.astype(BF16)
            all_grads[lines, own(1)] = nn(grad_score, block).astype(BF16)
        sums[SELF_BIAS + 1 : SELF_BIAS + 2, lanes] += value_sum
        for i in range(lines_count):
            met = reach(i)
            grad_score = jnp.concatenate([score_place(k, i - k)[...] for k in met], axis=0)
            made = diagonal(nn(turned[lanes, rows_of(met)], grad_score)).T * HEAD**-0.5
            sums[SELF_BIAS : SELF_BIAS + 1, lanes] += column_sum(made)
            all_grads[i * LINE : (i + 1) * LINE, own(0)] = made.astype(BF16)
        self_kept.next(pair)
        weight_grad(s_parts.at[pair], target, all_grads, 0, pair * 3 * PAIR, 3 * PAIR)
        for n in range(PAIRS):
            pl.when(pair == n)(functools.partial(every, part_sums[n], "begin"))

    loop(
        PAIRS,
        attend_back,
        at_step(0, (cross_sum[:1], "third"), (out_sum, "second"))
        + at_step(1, (cross_sum[:1], "fourth"), (out_sum, "third"), (part_sums[0], "second"))
        + at_step(2, (out_sum, "fourth"), (part_sums[0], "third"), (part_sums[1], "second"))
        + at_step(3, (part_sums[0], "fourth"), (part_sums[1], "third"), (part_sums[2], "second")),
    )

    row_moves = []
    row_moves = []
    row_moves = []

    def row_copy(slot, stage, peer):
        return pltpu.make_async_remote_copy(
            src_ref=row_send.at[stage],
            dst_ref=row_recv.at[slot],
            send_sem=v_send.at[slot],
            recv_sem=v_recv.at[slot],
            device_id=peer,
            device_id_type=MESH,
        )

    def row_go(slots, stage, peers):
        for slot, peer in zip(slots, peers):
            moving = row_copy(slot, stage, peer)
            moving.start()
            row_moves.append((slot, moving))

    def row_add(slots, stage):
        total = row_send[stage]
        for slot, moving in row_moves:
            if slot in slots:
                moving.wait_recv()
                total = total + row_recv[slot]
        return total

    if exchange:
        row_send[0] = sums[...]
        row_go([0], 0, [at.core_peer])
    final = copies.tiles(grad, target_grad_far, steps, TILE)
    memory_final = copies.tiles(dk, memory_grad_far, sources // TILE, TILE)

    def close(i):
        lines = part(i, TILE)
        made = grad[lines, :]
        for k in range(3):
            places = [(3 * p + k) * PAIR for p in range(PAIRS)]
            left = jnp.concatenate([all_grads[lines, a : a + PAIR] for a in places], axis=1)
            made = made + nt(left, matrix(s_qkv, k * width, width))
        grad[lines, :] = made
        final.start(i)

    def close_memory(i):
        lines = part(i, TILE)
        dk[lines, :] = nt(cross_dk_low[lines, :], matrix(c_qkv, width, width)) + nt(
            cross_dv_low[lines, :], matrix(c_qkv, 2 * width, width)
        )
        memory_final.start(i)

    loop(
        sources // TILE,
        close_memory,
        at_step(0, (part_sums[3], "second"), (part_sums[1], "fourth"))
        + at_step(1, (part_sums[2], "third")),
    )
    if exchange:
        row_send[1] = row_add([0], 0)
        row_go([1], 1, [at.x_peer])
    loop(steps, close, at_step(0, (part_sums[3], "third"), (part_sums[2], "fourth")))
    if exchange:
        row_send[2] = row_add([1], 1)
        row_go([2], 2, [at.y_peer])
    every(ff_sum, "last")
    every(cross_sum, "last")
    every(out_sum, "last")
    every(part_sums[3], "fourth")
    if exchange:
        slots = list(range(3, narrow + 2))
        row_send[3] = row_add([2], 2)
        row_go(slots, 3, at.z_peers)
    for group in part_sums:
        every(group, "last")
    if exchange:
        row_total[...] = row_add(slots, 3)
        for move in sums_out:
            move.close()
        for _, moving in row_moves:
            moving.wait_send()
    final.wait_all()
    memory_final.wait_all()
    copies.close()


def tail_kernel(narrow, *refs):
    refs = list(refs)
    take = lambda n: [refs.pop(0) for _ in range(n)]
    far_in = take(3 + 1 + SCATTERED)
    far_out = take(3 + WEIGHTS)
    s_bias, c_bias, gain_out, shift_out, in_bias, out_bias = take(6)
    near = take(3 + 1 + SCATTERED)
    joined, sems = take(2)
    copies = Copies(sems)
    wide = []
    piece = TILE // 2
    for source, buffer, out in zip(far_in[:3], near[:3], far_out[:3]):
        steps = buffer.shape[0] // piece
        entering = copies.tiles(source, buffer, steps, piece)
        entering.start_all()
        wide.append((steps, entering, copies.tiles(buffer, out, steps, piece)))
    plain = [copies.start(source, buffer) for source, buffer in zip(far_in[3:], near[3:])]
    for steps, entering, leaving in wide:
        for i in range(steps):
            entering.wait(i)
            leaving.start(i)
    copies.wait(*plain)
    for buffer, out in zip(near[4:9], far_out[3:8]):
        copies.start(buffer, out)
    for p, source in enumerate(near[9:]):
        for k in range(3):
            lanes = slice((k * PAIRS + p) * PAIR, (k * PAIRS + p + 1) * PAIR)
            joined[:, lanes] = source[:, k * PAIR : (k + 1) * PAIR]
    copies.start(joined, far_out[8])
    total = near[3][...]
    width = total.shape[1]
    devices = 8 * narrow
    index = lax.axis_index("wide") * narrow + lax.axis_index("narrow")
    each = width // devices
    own = pltpu.roll(total, lax.rem(width - index * each, width), 1)
    s_bias[...] = own[SELF_BIAS : SELF_BIAS + 3, :each]
    c_bias[...] = own[CROSS_BIAS : CROSS_BIAS + 3, :each]
    gain_out[...] = own[GAIN : GAIN + 3, :each]
    shift_out[...] = own[SHIFT : SHIFT + 3, :each]
    out_bias[...] = own[OUT_BIAS : OUT_BIAS + 1, :each]
    long = 4 * each
    in_row = devices // 4
    own = pltpu.roll(total, lax.rem(width - lax.rem(index, in_row) * long, width), 1)
    row = lax.broadcasted_iota(jnp.int32, own.shape, 0)
    own = column_sum(jnp.where(row == IN_BIAS + index // in_row, own, 0.0))
    in_bias[...] = own[:, :long]
    for _, _, leaving in wide:
        leaving.wait_all()
    copies.close()


def shape(dims, dtype):
    return jax.ShapeDtypeStruct(tuple(dims), dtype)


def whole(count):
    return [pl.BlockSpec(memory_space=pltpu.VMEM)] * count


def far(count):
    return [pl.BlockSpec(memory_space=pl.ANY)] * count


def scalars(count):
    return [pl.BlockSpec(memory_space=pltpu.SMEM)] * count


def cut(rows, columns):
    return (2, 2, 2, rows // 8, columns)


def local(wide, narrow, *args):
    target, memory, cotangent, target_lengths, source_lengths = args[:5]
    self_qkv, self_out, self_bias, cross_qkv, cross_out, cross_bias = args[5:11]
    ff_in, ff_in_bias, ff_out, ff_out_bias, ln_gain, ln_bias = args[11:]
    rows, width = target.shape
    sources = memory.shape[0]
    hidden = ff_in.shape[1]
    lines = rows // LINE
    axes = ("wide", "narrow")
    exchange = wide == 8 and narrow == 4 and self_qkv.shape[0] % 16 == 0
    weights = [self_qkv, self_out, cross_qkv, cross_out, ff_in, ff_out]

    def params(number):
        if exchange and number is not None:
            return pltpu.CompilerParams(
                collective_id=number, has_side_effects=True, vmem_limit_bytes=VMEM_BYTES
            )
        return pltpu.CompilerParams(vmem_limit_bytes=VMEM_BYTES)

    wide_outs = [
        shape((rows, width), BF16),
        shape((sources, width), F32),
        shape((rows, width), F32),
    ]
    table = shape((VECTORS, width), F32)
    partial_sums = [
        shape(cut(hidden, width), BF16),
        shape(cut(width, hidden), BF16),
        shape(cut(width, 3 * width), BF16),
        shape(cut(width, width), BF16),
        shape(cut(width, width), BF16),
        shape((PAIRS,) + cut(width, 3 * width // PAIRS), BF16),
        table,
    ]
    row_block = shape((rows, width), BF16)
    source_block = shape((sources, width), BF16)
    row_sums = shape((lines, HEADS, LINE), F32)
    scratch = [shape(cut(w.shape[0] * wide * narrow, w.shape[1]), BF16) for w in weights]
    scratch += [row_block, source_block] + [row_block] * 5
    scratch += [row_block, source_block, source_block, row_block]
    scratch += [shape((rows, width), F32), shape((rows, LINE), F32)]
    scratch += [
        shape((width, rows), BF16),
        shape((rows, LINE), BF16),
        shape((sources, LINE), BF16),
        shape((rows, LINE), BF16),
        shape((rows, hidden), BF16),
        shape((rows, hidden), BF16),
        row_block,
        row_block,
        row_block,
        row_block,
        row_sums,
        row_sums,
        row_sums,
        shape((2 * rows, PAIR), BF16),
        shape((2 * rows, PAIR), BF16),
        shape((rows, width), F32),
        shape((sources, width), F32),
        shape((sources, width), F32),
        shape((rows, LINE), F32),
    ]
    outs = list(wide_outs)
    if exchange:
        shorts = [self_bias, cross_bias, ln_gain, ln_bias]
        shorts += [ff_out_bias[None, :], ff_in_bias[None, :]]
        given = weights + shorts
        specs = far(len(weights)) + whole(len(shorts))
        own = [ff_out, ff_in, cross_qkv, cross_out, self_out]
        outs += [shape(w.shape, F32) for w in own]
        outs += [shape((self_qkv.shape[0], 3 * width // PAIRS), F32)] * PAIRS
        scattered = outs[3:]
        outs.append(table)
        scratch = partial_sums[2:] + scratch
    else:
        gathered = [lax.all_gather(w, axes, axis=0, tiled=True) for w in weights]
        short_rows = [self_bias, cross_bias, ln_gain, ln_bias, ff_out_bias[None, :]]
        vec = jnp.concatenate(
            [lax.all_gather(v, axes, axis=1, tiled=True) for v in short_rows], axis=0
        )
        last = lax.all_gather(ff_in_bias, axes, axis=0, tiled=True).reshape(-1, width)
        vec = jnp.concatenate([vec, last], axis=0).astype(F32)
        vec = jnp.pad(vec, ((0, VECTORS - vec.shape[0]), (0, 0)))
        given = [w.reshape(cut(*w.shape)) for w in gathered] + [vec]
        specs = far(len(weights)) + whole(1)
        outs += partial_sums
    outs.append(shape((PAIRS, rows, REACH * 2 * LINE), BF16))
    outs.append(shape((PAIRS * lines // GROUP, sources, GROUP * 2 * LINE), BF16))
    buffers = [pltpu.VMEM(x.shape, x.dtype) for x in scratch]
    buffers.append(pltpu.SemaphoreType.DMA((Copies.COUNT,)))
    if exchange:
        buffers += [
            pltpu.VMEM((VECTORS, width), F32),
            pltpu.VMEM(cut(16 * wide * narrow, 256), BF16),
            pltpu.VMEM((16, 256), F32),
            pltpu.VMEM((16, 256), BF16),
        ]
        buffers += [pltpu.SemaphoreType.DMA((GATHERED, narrow + 4))] * 2
        for w in scattered:
            buffers += Scatter.scratch(w.shape[0], w.shape[1], narrow)
        buffers += [
            pltpu.VMEM((4, VECTORS, width), F32),
            pltpu.VMEM((narrow + 2, VECTORS, width), F32),
        ]
        buffers += [pltpu.SemaphoreType.DMA((SCATTERED, narrow + 4))] * 2
        buffers += [pltpu.SemaphoreType.DMA((narrow + 2,))] * 2
    made = pl.pallas_call(
        functools.partial(layer_kernel, exchange, narrow),
        out_shape=outs,
        in_specs=scalars(2) + far(3) + specs,
        out_specs=far(3) + whole(len(outs) - 5) + far(2),
        scratch_shapes=buffers,
        compiler_params=params(0),
        name="layer",
    )(target_lengths, source_lengths, target, memory, cotangent, *given)
    if exchange:
        own.append(self_qkv)
        outs = wide_outs + [shape(w.shape, F32) for w in own]
        outs += [
            shape(self_bias.shape, F32),
            shape(cross_bias.shape, F32),
            shape(ln_gain.shape, F32),
            shape(ln_bias.shape, F32),
            shape((1, ff_in_bias.shape[0]), F32),
            shape((1, ff_out_bias.shape[0]), F32),
        ]
        made = pl.pallas_call(
            functools.partial(tail_kernel, narrow),
            out_shape=outs,
            in_specs=far(4 + SCATTERED),
            out_specs=far(3 + WEIGHTS) + whole(6),
            scratch_shapes=[
                pltpu.VMEM(x.shape, x.dtype) for x in wide_outs + [table] + scattered
            ]
            + [pltpu.VMEM(self_qkv.shape, F32), pltpu.SemaphoreType.DMA((Copies.COUNT,))],
            compiler_params=params(None),
            name="tail",
        )(*made[:3], made[3 + SCATTERED], *made[3 : 3 + SCATTERED])
    output, memory_grad, target_grad = made[:3]
    if exchange:
        f_out_sum, f_in_sum, c_qkv_sum, c_out_sum, s_out_sum, s_qkv_sum = made[3:9]
        s_bias_sum, c_bias_sum, gain_sum, shift_sum, in_bias_sum, out_bias_sum = made[9:]
        in_bias_sum = in_bias_sum.reshape(-1)
        out_bias_sum = out_bias_sum.reshape(-1)
    else:

        def spread(value):
            value = value.reshape(-1, value.shape[-1]).astype(F32)
            return lax.psum_scatter(value, axes, scatter_dimension=0, tiled=True)

        def spread_row(value):
            return lax.psum_scatter(value, axes, scatter_dimension=value.ndim - 1, tiled=True)

        f_out_sum, f_in_sum, c_qkv_sum, c_out_sum, s_out_sum = [spread(v) for v in made[3:8]]
        pieces = [spread(made[8][n]).reshape(-1, 3, width // PAIRS) for n in range(PAIRS)]
        s_qkv_sum = jnp.concatenate(pieces, axis=2).reshape(-1, 3 * width)
        sums = made[9]
        s_bias_sum = spread_row(sums[SELF_BIAS : SELF_BIAS + 3])
        c_bias_sum = spread_row(sums[CROSS_BIAS : CROSS_BIAS + 3])
        gain_sum = spread_row(sums[GAIN : GAIN + 3])
        shift_sum = spread_row(sums[SHIFT : SHIFT + 3])
        out_bias_sum = spread_row(sums[OUT_BIAS])
        in_bias_sum = spread_row(sums[IN_BIAS : IN_BIAS + hidden // width].reshape(-1))
    return (
        output,
        target_grad,
        memory_grad,
        s_qkv_sum,
        s_out_sum,
        s_bias_sum,
        c_qkv_sum,
        c_out_sum,
        c_bias_sum,
        f_in_sum,
        in_bias_sum,
        f_out_sum,
        out_bias_sum,
        gain_sum,
        shift_sum,
    )


def solution(mesh):
    rows = P(("wide", "narrow"), None)
    columns = P(None, ("wide", "narrow"))
    flat = P(("wide", "narrow"))
    return jax.shard_map(
        functools.partial(local, mesh.shape["wide"], mesh.shape["narrow"]),
        mesh=mesh,
        in_specs=(
            rows,
            rows,
            rows,
            rows,
            rows,
            rows,
            rows,
            columns,
            rows,
            rows,
            columns,
            rows,
            flat,
            rows,
            flat,
            columns,
            columns,
        ),
        out_specs=(
            rows,
            rows,
            rows,
            rows,
            rows,
            columns,
            rows,
            rows,
            columns,
            rows,
            flat,
            rows,
            flat,
            columns,
            columns,
        ),
        check_vma=False,
    )
```
